32 devices in a mesh: groups: 2 (over y), tiles: 4 (over z), feat: 2 (over x), rep: 2 (over core).
Axes of the slice: x: 2, y: 2, z: 4, core: 2. Of those that a mesh axis runs over, the one named last changes fastest.
Arguments:
- points: bfloat16 [65536, 512], P(('groups', 'tiles', 'rep')), parts along dimension 0, may hold values from -6 to 6
- dest_tile: int32 [65536, 1], P(('groups', 'tiles', 'rep')), parts along dimension 0, may hold values from 0 to 3; in each aligned block of 4096 rows (0 to 4095, 4096 to 8191, ...) at most 3072 rows name the same one
- member: int32 [65536], P(('groups', 'tiles', 'rep')), parts along dimension 0, may hold values from 0 to 255
- w_point: bfloat16 [512, 512], P(None, 'feat'), may hold values from -0.25 to 0.25
- ln_gain: float32 [512], replicated, may hold values from 0.5 to 1.5
- w_qkv: bfloat16 [3, 512, 512], P(None, None, 'feat'), may hold values from -0.25 to 0.25
- temper: float32 [8], P('feat'), may hold values from 4 to 12
- w_out: bfloat16 [512, 512], P('feat'), may hold values from -0.25 to 0.25
- adjacency: int32 [16, 4], P(('groups', 'tiles', 'rep')), parts along dimension 0, may hold values 0 or 1
Outputs:
- states: bfloat16 [2048, 512], P(('groups', 'tiles', 'rep'), 'feat'), parts along dimension 0
The draws below stay inside these ranges and needn't reach their ends.
There are 2 independent parts, one for each index of `groups`. The reference program is written for one: setup_inputs(seed, part) draws one part's arguments, and reference() takes and returns one part's arrays. A program takes and returns all parts, laid end to end along the dimension named above; an argument that names none is the same for every part. Nothing has to cross between parts.
Inputs may be any that keep to these rules, and one draw needn't show every extreme that they name: `dest_tile`: no more than 3072 rows of one device name one tile; in every draw some device sends exactly 3072 rows to some tile.
All inputs are finite; a program needn't handle non-finite values. No bound on the sum of `adjacency` on one device may be relied on, other than what follows from the above.
Results may differ from the reference program's by a relative error of at most 0.008.
Values may be sent and summed in bfloat16 or wider, within the bound.
A program may use at most 64 MiB of HBM per device.

```python
import math
import jax
import jax.numpy as jnp
import numpy as np
from jax import lax

D = 512
H = 8
HS = 64
P_DEV = 4096
S_BLK = 128
REACH = 2
S_TILE = 256
NB = 8
CAP = 3072
POINTS = 32768
N_TILES = 4


def place_ends(drawn, stream_key, least, high):
    shape = drawn.shape
    index_at = [jax.random.randint(jax.random.fold_in(stream_key, axis), (), 0, shape[axis]) for axis in range(len(shape))]
    drawn = drawn.at[tuple(index_at)].set(least)
    longest = shape.index(max(shape))
    index_at[longest] = (index_at[longest] + 1) % shape[longest]
    return drawn.at[tuple(index_at)].set(high)


def block_scale(stream_key, extent, split, smallest, high):
    factor_of = 1.0
    for position, parts in split:
        draws = jax.random.uniform(jax.random.fold_in(jax.random.fold_in(stream_key, 6), position), (parts,), jnp.float32, smallest / len(split), high / len(split))
        factor_of = factor_of * jnp.repeat(jnp.exp(draws), extent[position] // parts).reshape((-1,) + (1,) * (len(extent) - 1 - position))
    return factor_of


def cumulative_ranks(count, lean):
    loads = [(1 << 20) // math.isqrt(rank ** lean) + 1 for rank in range(1, count + 1)]
    spread = 1 + sum(loads) // (1 << 30)
    return np.cumsum(np.array([max(1, weight // spread) for weight in loads]))


def ranked_ids(rng, dims, count, skew):
    grid = cumulative_ranks(count, skew)
    pick = jax.random.randint(jax.random.fold_in(rng, 1), dims, 0, int(grid[count - 1]))
    grade = jnp.searchsorted(jnp.asarray(grid, jnp.int32), pick, side="right")
    return jax.random.permutation(jax.random.fold_in(rng, 2), count)[grade].astype(jnp.int32)


def deal_out(stream_key, own, number, rows, amount, top, most, lean):
    sequence = jax.random.permutation(stream_key, amount)
    crowded, common = load_shares(amount, rows * top, most, lean, True), load_shares(amount, rows * top, most, lean, False)
    places = jnp.arange(amount)

    def named(tallies, turn):
        used = int((tallies > 0).sum())
        fixed = max(1, used // 4)
        moved = fixed + (places - fixed + turn * (used - fixed)) % max(1, amount - fixed)
        return jnp.zeros((amount,), jnp.int32).at[sequence[jnp.where(places < fixed, places, moved)]].set(jnp.asarray(tallies, jnp.int32))

    tallies = jnp.where(number % 4 == 0, named(crowded, number // 4), named(common, number - number // 4 - 1))
    mixed = jax.random.permutation(jax.random.fold_in(own, 3), amount)
    giver, taker = mixed[0:amount // 2 * 2:2], mixed[1:amount // 2 * 2:2]
    slack = jnp.minimum(tallies[giver] - 1, most - tallies[taker]) // 2
    slack = jnp.where((giver == sequence[0]) | (taker == sequence[0]) | (tallies[taker] == 0), 0, jnp.maximum(slack, 0))
    moved = jax.random.randint(jax.random.fold_in(own, 4), (amount // 2,), 0, 1 << 20) % (slack + 1)
    tallies = tallies.at[giver].add(-moved).at[taker].add(moved)
    items = jnp.searchsorted(jnp.cumsum(tallies), jnp.arange(rows * top), side="right").astype(jnp.int32)
    grid = items.reshape(top, rows).T
    grid = grid[jax.random.permutation(jax.random.fold_in(own, 1), rows)]
    turn = jax.random.randint(jax.random.fold_in(own, 2), (rows, 1), 0, top)
    return jnp.take_along_axis(grid, (jnp.arange(top)[None, :] + turn) % top, axis=1)


def load_shares(count, total, most, skew, full):
    loads = [(1 << 20) // math.isqrt(rank ** skew) + 1 for rank in range(1, count + 1)]
    largest = most if full else min(most, max(-(-total // count), total * loads[0] // sum(loads)))
    least = 1 if total - largest >= count - 1 else 0
    counts, surplus = [largest] + [least] * (count - 1), total - largest - least * (count - 1)
    while surplus > 0:
        movable = [i for i in range(1, count) if counts[i] < largest] or [i for i in range(1, count) if counts[i] < most]
        whole, budget = sum([loads[i] for i in movable]), surplus
        for i in movable:
            extra = min(most - counts[i], max(1, budget * loads[i] // whole), surplus)
            counts[i] = counts[i] + extra
            surplus = surplus - extra
    return np.array(counts)


def normal_values(key, shape, spread, bound, pieces=(), kind=jnp.bfloat16):
    array = jax.random.normal(key, shape, jnp.float32) * spread
    if len(pieces) > 0:
        array = block_scale(key, shape, pieces, -0.22, 0.18) * array
    return jnp.clip(array, min=-bound, max=bound).astype(kind)


def setup_inputs(seed: int = 0, part: int = 0) -> dict:
    seeds = jax.random.split(jax.random.key(seed), 10)
    own_keys = jax.random.split(jax.random.fold_in(seeds[9], part), 10)
    points = normal_values(own_keys[0], (POINTS, D), 1.0, 6.0, ((0, 8),))
    dest_tile_keys = jax.random.split(jax.random.fold_in(own_keys[1], 1), POINTS // P_DEV)
    dest_tile_turns = jax.random.permutation(jax.random.fold_in(own_keys[1], 3), POINTS // P_DEV)
    dest_tile = jax.vmap(lambda own, number: deal_out(jax.random.fold_in(own_keys[1], 2), own, number, P_DEV, N_TILES, 1, CAP, 2))(dest_tile_keys, dest_tile_turns).reshape((POINTS, 1))
    member = place_ends(ranked_ids(own_keys[2], (POINTS,), S_TILE, 2), jax.random.fold_in(own_keys[2], 3), 0, S_TILE - 1).astype(jnp.int32)
    w_point = normal_values(seeds[3], (D, D), D ** -0.5, 0.25, ((1, 2),))
    ln_gain = jnp.clip(1.0 + 0.1 * jax.random.normal(seeds[4], (D,), jnp.float32), 0.5, 1.5)
    w_qkv = normal_values(seeds[5], (3, D, D), D ** -0.5, 0.25, ((2, 2),))
    temper = jnp.clip(jnp.exp(math.log(12.0) - 1.0986123 * jax.random.uniform(seeds[6], (H,), jnp.float32) ** block_scale(seeds[6], (H,), ((0, 2),), -0.2, 0.2)), 4.0, 12.0)
    w_out = normal_values(seeds[7], (D, D), D ** -0.5, 0.25, ((0, 2),))
    adjacency = place_ends((jax.random.randint(own_keys[8], (NB, 2 * REACH), 0, 4) < 3).astype(jnp.int32), jax.random.fold_in(own_keys[8], 1), 0, 1)
    return {"points": points, "dest_tile": dest_tile, "member": member, "w_point": w_point, "ln_gain": ln_gain, "w_qkv": w_qkv, "temper": temper, "w_out": w_out, "adjacency": adjacency}


def unit_heads(proj):
    return proj * lax.rsqrt(lax.optimization_barrier(jnp.sum(proj * proj, axis=-1, keepdims=True)) + 1e-06)

def reference(points, dest_tile, member, w_point, ln_gain, w_qkv, temper, w_out, adjacency):
    hidden = jax.nn.gelu(jnp.dot(points, w_point, preferred_element_type=jnp.float32)).astype(jnp.bfloat16)
    owner = (dest_tile[:, 0] * S_TILE + member).astype(jnp.int32)
    total = NB * S_BLK
    sums = jax.ops.segment_sum(hidden.astype(jnp.float32), owner, num_segments=total)
    count = jax.ops.segment_sum(jnp.ones(owner.shape, jnp.float32), owner, num_segments=total)
    pooled = (sums / jnp.maximum(count, 1.0)[:, None]).astype(jnp.bfloat16)
    lifted = pooled.astype(jnp.float32)
    mean = lax.optimization_barrier(jnp.mean(lifted, axis=1, keepdims=True))
    var = lax.optimization_barrier(jnp.mean((lifted - mean) ** 2, axis=1, keepdims=True))
    normed = ((lifted - mean) * lax.rsqrt(var + 1e-05) * ln_gain.astype(jnp.float32)).astype(jnp.bfloat16)
    proj = jnp.einsum('sd,ide->ise', normed.astype(jnp.float32), w_qkv.astype(jnp.float32))
    proj = proj.reshape(3, total, H, HS)
    query = unit_heads(proj[0]).astype(jnp.bfloat16).reshape(NB, S_BLK, H, HS)
    key = unit_heads(proj[1]).astype(jnp.bfloat16).reshape(NB, S_BLK, H, HS)
    value = proj[2].astype(jnp.bfloat16).reshape(NB, S_BLK, H, HS)
    zeros = jnp.zeros((REACH, S_BLK, H, HS), jnp.bfloat16)
    key_pad = jnp.concatenate([zeros, key, zeros], axis=0)
    value_pad = jnp.concatenate([zeros, value, zeros], axis=0)
    offsets = [0] + list(range(-REACH, 0)) + list(range(1, REACH + 1))
    cand_key = jnp.stack([key_pad[REACH + o:REACH + o + NB] for o in offsets], axis=1)
    cand_value = jnp.stack([value_pad[REACH + o:REACH + o + NB] for o in offsets], axis=1)
    width = len(offsets) * S_BLK
    cand_key = cand_key.reshape(NB, width, H, HS)
    cand_value = cand_value.reshape(NB, width, H, HS)
    block_ids = jnp.arange(NB, dtype=jnp.int32)
    columns = [jnp.ones((NB,), jnp.float32)]
    for j in range(2 * REACH):
        shift_by = offsets[j + 1]
        inside = (block_ids + shift_by >= 0) & (block_ids + shift_by < NB) & (adjacency[:, j] == 1)
        columns.append(inside.astype(jnp.float32))
    keymask = jnp.repeat(jnp.stack(columns, axis=1), S_BLK, axis=1)
    scores = jnp.einsum('bqhd,bkhd->bhqk', query.astype(jnp.float32), cand_key.astype(jnp.float32))
    scores = scores * temper.astype(jnp.float32)[None, :, None, None]
    expd = jnp.exp(scores) * keymask[:, None, None, :]
    probs = (expd / lax.optimization_barrier(jnp.sum(expd, axis=-1, keepdims=True))).astype(jnp.bfloat16)
    attended = jnp.einsum('bhqk,bkhd->bqhd', probs.astype(jnp.float32), cand_value.astype(jnp.float32))
    attended = attended.astype(jnp.bfloat16).reshape(total, D)
    mixed = pooled.astype(jnp.float32) + jnp.dot(attended, w_out, preferred_element_type=jnp.float32)
    return mixed.astype(jnp.bfloat16)
```

```python
import functools

import jax
import jax.numpy as jnp
from jax import lax
from jax.experimental import pallas as pl
from jax.experimental.pallas import tpu as pltpu
from jax.sharding import PartitionSpec as P

S_BLK = 128
REACH = 2
HEAD = 64
CHUNK = 1024
MESH = pl.DeviceIdType.MESH
OFFSETS = tuple(range(-REACH, 0)) + tuple(range(1, REACH + 1))
NT = (((1,), (1,)), ((), ()))
F32 = jnp.float32
BF16 = jnp.bfloat16


def loop(count, step):
    if count <= 8:
        for k in range(count):
            step(k)
    else:
        lax.fori_loop(0, count, lambda k, c: (step(k), c)[1], 0)


def kernel(
    T, R, F, H,
    dest_ref, member_ref, temper_ref, adj_ref, gain_ref, points_hbm, wp_hbm, wqkv_hbm, wo_hbm,
    out_ref,
    pts, wp, wqkv, wo, hid, moh, cnt_send, cnt_recv, tsum, rep_send, rep_recv, z_send, z_recv,
    pool, kv_own, kv_recv, att, qm, lsum, acc,
    in_sem, wo_ss, wo_rs, cnt_ss, cnt_rs, rep_ss, rep_rs, z_ss, z_rs, pool_ss, pool_rs,
    kv_ss, kv_rs, att_ss, att_rs,
):
    t, r, f = lax.axis_index("tiles"), lax.axis_index("rep"), lax.axis_index("feat")
    other = 1 - r
    rows = pts.shape[0]
    dim = pts.shape[1]
    wid = wp.shape[1]
    chunks = rows // CHUNK
    blocks = T * R
    block = t * R + r

    loads = [pltpu.make_async_copy(wp_hbm, wp, in_sem.at[chunks])]
    for c in range(chunks):
        part = pl.ds(c * CHUNK, CHUNK)
        loads.append(pltpu.make_async_copy(points_hbm.at[part], pts.at[part], in_sem.at[c]))
    loads.append(pltpu.make_async_copy(wqkv_hbm, wqkv, in_sem.at[chunks + 1]))
    my_cols = pl.ds(pl.multiple_of(f * wid, 128), wid)
    loads.append(pltpu.make_async_copy(wo_hbm.at[:, my_cols], wo.at[f], in_sem.at[chunks + 2]))
    for load in loads:
        load.start()

    barrier = pltpu.get_barrier_semaphore()

    def greet(i):
        pl.semaphore_signal(
            barrier, inc=1, device_id={"tiles": lax.rem(t + i, T), "rep": r}, device_id_type=MESH
        )
        pl.semaphore_signal(
            barrier, inc=1, device_id={"tiles": lax.rem(t + i, T), "rep": other},
            device_id_type=MESH,
        )

    loop(T - 1, lambda k: greet(k + 1))
    pl.semaphore_signal(barrier, inc=1, device_id={"rep": other}, device_id_type=MESH)
    for i in range(1, F):
        pl.semaphore_signal(
            barrier, inc=1, device_id={"feat": lax.rem(f + i, F)}, device_id_type=MESH
        )

    t_rows = max(T, 16)
    counts = jnp.zeros((t_rows, R * S_BLK), F32)
    for c in range(chunks):
        cols = pl.ds(c * CHUNK, CHUNK)
        ids = lax.broadcasted_iota(jnp.int32, (R * S_BLK, CHUNK), 0)
        hot = jnp.where(ids == member_ref[:, cols], 1.0, 0.0).astype(BF16)
        moh[:, cols] = hot
        tids = lax.broadcasted_iota(jnp.int32, (t_rows, CHUNK), 0)
        thot = jnp.where(tids == dest_ref[:, cols], 1.0, 0.0).astype(BF16)
        counts += lax.dot_general(thot, hot, NT, preferred_element_type=F32)
    for i in range(T):
        for j in range(R):
            cnt_send[i, j] = jnp.broadcast_to(
                counts[i : i + 1, j * S_BLK : (j + 1) * S_BLK], (8, S_BLK)
            )

    pl.semaphore_wait(barrier, R * T - 1 + F - 1)

    def remote(src, dst, ss, rs, device):
        return pltpu.make_async_remote_copy(
            src_ref=src, dst_ref=dst, send_sem=ss, recv_sem=rs, device_id=device,
            device_id_type=MESH,
        )

    def wo_copy(i):
        p = lax.rem(f + i, F)
        cols = pl.ds(pl.multiple_of(p * wid, 128), wid)
        return remote(wo_hbm.at[:, cols], wo.at[f], wo_ss.at[p], wo_rs.at[f], {"feat": p})

    def cnt_copy(i, j):
        p = lax.rem(t + i, T)
        return remote(
            cnt_send.at[p, j], cnt_recv.at[t, r], cnt_ss.at[p, j], cnt_rs.at[t, r],
            {"tiles": p, "rep": j},
        )

    loop(T - 1, lambda k: (cnt_copy(k + 1, r).start(), cnt_copy(k + 1, other).start()))
    cnt_copy(0, other).start()
    for i in range(1, F):
        wo_copy(i).start()

    loads[0].wait()
    for c in range(chunks):
        loads[1 + c].wait()
        part = pl.ds(c * CHUNK, CHUNK)
        x = jnp.dot(pts[part], wp[...], preferred_element_type=F32)
        inner = 0.7978845608028654 * (x + 0.044715 * (x * x * x))
        hid[part] = (0.5 * x * (1.0 + jnp.tanh(inner))).astype(BF16)

    def tile_at(k):
        return lax.rem(t + 1 + lax.rem(T // 2 - 1 - k + (T - 1), T - 1), T)

    def rep_copy(k):
        return remote(
            rep_send.at[k], rep_recv.at[k], rep_ss.at[k], rep_rs.at[k], {"rep": other}
        )

    def z_copy(k):
        return remote(
            z_send.at[k], z_recv.at[t], z_ss.at[k], z_rs.at[t], {"tiles": tile_at(k)}
        )

    def sum_tile(k, tile):
        here = jnp.where(dest_ref[...] == tile, 1.0, 0.0).astype(BF16)
        sums = jnp.dot(moh[...] * here, hid[...], preferred_element_type=F32)
        for j in range(R):
            tsum[k, j] = sums[j * S_BLK : (j + 1) * S_BLK]
        rep_send[k] = tsum[k, other].astype(BF16)
        rep_copy(k).start()

    def pass_on(k):
        rep_copy(k).wait_recv()
        z_send[k] = (tsum[k, r] + rep_recv[k].astype(F32)).astype(BF16)
        z_copy(k).start()

    sum_tile(0, tile_at(0))

    def middle(k):
        sum_tile(k + 1, tile_at(k + 1))
        pass_on(k)

    loop(T - 2, middle)
    sum_tile(T - 1, t)
    pass_on(T - 2)

    cnt_recv[t, r] = cnt_send[t, r]

    def cnt_wait(i, j):
        p = lax.rem(t + i, T)
        remote(
            cnt_send.at[p, j], cnt_recv.at[p, j], cnt_ss.at[p, j], cnt_rs.at[p, j],
            {"tiles": p, "rep": j},
        ).wait_recv()

    loop(T - 1, lambda k: (cnt_wait(k + 1, r), cnt_wait(k + 1, other)))
    cnt_wait(0, other)
    total = jnp.sum(cnt_recv[...].reshape(blocks, 8, S_BLK), axis=0)
    column = jnp.transpose(jnp.broadcast_to(total[0:1], (S_BLK, S_BLK)))
    column = jnp.maximum(column, 1.0)

    rep_copy(T - 1).wait_recv()
    tsum[T - 1, r] += rep_recv[T - 1].astype(F32)

    def gather_sum(i):
        p = lax.rem(t + i, T)
        remote(z_send.at[0], z_recv.at[p], z_ss.at[0], z_rs.at[p], {"tiles": p}).wait_recv()
        tsum[T - 1, r] += z_recv[p].astype(F32)

    loop(T - 1, lambda k: gather_sum(k + 1))
    sums = tsum[T - 1, r]
    pooled = jnp.concatenate(
        [sums[:, g * 128 : (g + 1) * 128] / column for g in range(wid // 128)], axis=1
    ).astype(BF16)
    pool[f] = pooled

    def feat_copy(ref, ss, rs, i):
        p = lax.rem(f + i, F)
        return remote(ref.at[f], ref.at[f], ss.at[p], rs.at[f], {"feat": p})

    def feat_wait(ref, ss, rs, i):
        p = lax.rem(f + i, F)
        remote(ref.at[p], ref.at[p], ss.at[p], rs.at[p], {"feat": p}).wait_recv()

    for i in range(1, F):
        feat_copy(pool, pool_ss, pool_rs, i).start()
    loads[chunks + 1].wait()
    for i in range(1, F):
        feat_wait(pool, pool_ss, pool_rs, i)

    lifted = jnp.concatenate([pool[p].astype(F32) for p in range(F)], axis=1)
    mean = jnp.sum(lifted, axis=1, keepdims=True) * (1.0 / dim)
    centred = lifted - mean
    var = jnp.sum(centred * centred, axis=1, keepdims=True) * (1.0 / dim)
    normed = (centred * lax.rsqrt(var + 1e-05) * gain_ref[...]).astype(BF16)

    same_head = (
        lax.broadcasted_iota(jnp.int32, (wid, wid), 0) // HEAD
        == lax.broadcasted_iota(jnp.int32, (wid, wid), 1) // HEAD
    )
    spread = jnp.where(same_head, 1.0, 0.0).astype(BF16)

    def project(i):
        return jnp.dot(normed, wqkv[i], preferred_element_type=F32)

    def unit(proj):
        square = proj * proj
        high = square.astype(BF16)
        low = (square - high.astype(F32)).astype(BF16)
        norm = jnp.dot(high, spread, preferred_element_type=F32) + jnp.dot(
            low, spread, preferred_element_type=F32
        )
        return (proj * lax.rsqrt(norm + 1e-06)).astype(BF16)

    def inside(offset):
        return (block + offset >= 0) & (block + offset < blocks)

    def kv_copy(i, j):
        slot = len(OFFSETS) - 1 - j
        goal = block + OFFSETS[j]
        return remote(
            kv_own.at[i], kv_recv.at[slot, i], kv_ss.at[j, i], kv_rs.at[slot, i],
            {"tiles": goal // R, "rep": lax.rem(goal, R)},
        )

    def kv_wait(i, j):
        goal = block + OFFSETS[j]
        remote(
            kv_own.at[i], kv_recv.at[j, i], kv_ss.at[j, i], kv_rs.at[j, i],
            {"tiles": goal // R, "rep": lax.rem(goal, R)},
        ).wait_recv()

    def send_kv(i):
        for j in (0, len(OFFSETS) - 1, 1, 2):
            @pl.when(inside(OFFSETS[j]))
            def _():
                kv_copy(i, j).start()

    kv_own[0] = unit(project(1))
    send_kv(0)
    kv_own[1] = project(2).astype(BF16)
    send_kv(1)
    query = unit(project(0))
    lane_head = lax.broadcasted_iota(jnp.int32, (S_BLK, wid), 1) // HEAD
    for h in range(H):
        qm[h * S_BLK : (h + 1) * S_BLK] = jnp.where(lane_head == h, query, jnp.zeros_like(query))

    def attend(keys, values, mask, first):
        scores = lax.dot_general(qm[...], keys, NT, preferred_element_type=F32)
        expd = jnp.concatenate(
            [
                jnp.exp(scores[h * S_BLK : (h + 1) * S_BLK] * temper_ref[h])
                for h in range(H)
            ],
            axis=0,
        )
        if mask is not None:
            expd = expd * mask
        got = jnp.dot(expd.astype(BF16), values, preferred_element_type=F32)
        if first:
            lsum[...] = expd
            acc[...] = got
        else:
            lsum[...] += expd
            acc[...] += got

    attend(kv_own[0], kv_own[1], None, True)
    for j in (1, 2, 0, 3):
        @pl.when(inside(OFFSETS[j]))
        def _():
            kv_wait(0, j)
            kv_wait(1, j)
            mask = jnp.where(adj_ref[0, j] == 1, 1.0, 0.0).astype(F32)
            attend(kv_recv[j, 0], kv_recv[j, 1], mask, False)

    attended = jnp.zeros((S_BLK, wid), F32)
    for h in range(H):
        part = slice(h * S_BLK, (h + 1) * S_BLK)
        scale = 1.0 / jnp.sum(lsum[part], axis=1, keepdims=True)
        attended = jnp.where(lane_head == h, acc[part] * scale, attended)
    att[f] = attended.astype(BF16)
    for i in range(1, F):
        feat_copy(att, att_ss, att_rs, i).start()
    loads[chunks + 2].wait()
    mixed = pool[f].astype(F32) + jnp.dot(att[f], wo[f], preferred_element_type=F32)
    for i in range(1, F):
        p = lax.rem(f + i, F)
        remote(wo.at[p], wo.at[p], wo_ss.at[p], wo_rs.at[p], {"feat": p}).wait_recv()
        feat_wait(att, att_ss, att_rs, i)
        mixed += jnp.dot(att[p], wo[p], preferred_element_type=F32)
    out_ref[...] = mixed.astype(out_ref.dtype)

    loop(T - 1, lambda k: (cnt_copy(k + 1, r).wait_send(), cnt_copy(k + 1, other).wait_send()))
    cnt_copy(0, other).wait_send()
    loop(T, lambda k: rep_copy(k).wait_send())
    loop(T - 1, lambda k: z_copy(k).wait_send())
    for i in range(1, F):
        wo_copy(i).wait_send()
        feat_copy(pool, pool_ss, pool_rs, i).wait_send()
        feat_copy(att, att_ss, att_rs, i).wait_send()
    for j in range(len(OFFSETS)):
        @pl.when(inside(OFFSETS[j]))
        def _():
            kv_copy(0, j).wait_send()
            kv_copy(1, j).wait_send()


def body(points, dest_tile, member, w_point, ln_gain, w_qkv, temper, w_out, adjacency):
    T, R, F = lax.axis_size("tiles"), lax.axis_size("rep"), lax.axis_size("feat")
    H = temper.shape[0]
    rows, dim = points.shape
    wid = w_point.shape[1]
    near = len(OFFSETS)
    vmem = pl.BlockSpec(memory_space=pltpu.VMEM)
    smem = pl.BlockSpec(memory_space=pltpu.SMEM)
    anyw = pl.BlockSpec(memory_space=pl.ANY)
    dma = pltpu.SemaphoreType.DMA
    return pl.pallas_call(
        functools.partial(kernel, T, R, F, H),
        out_shape=jax.ShapeDtypeStruct((S_BLK, wid), BF16),
        in_specs=[vmem, vmem, smem, smem, vmem, anyw, anyw, anyw, anyw],
        out_specs=vmem,
        scratch_shapes=[
            pltpu.VMEM((rows, dim), BF16),
            pltpu.VMEM((dim, wid), BF16),
            pltpu.VMEM((3, dim, wid), BF16),
            pltpu.VMEM((F, wid, wid), BF16),
            pltpu.VMEM((rows, wid), BF16),
            pltpu.VMEM((R * S_BLK, rows), BF16),
            pltpu.VMEM((T, R, 8, S_BLK), F32),
            pltpu.VMEM((T, R, 8, S_BLK), F32),
            pltpu.VMEM((T, R, S_BLK, wid), F32),
            pltpu.VMEM((T, S_BLK, wid), BF16),
            pltpu.VMEM((T, S_BLK, wid), BF16),
            pltpu.VMEM((T, S_BLK, wid), BF16),
            pltpu.VMEM((T, S_BLK, wid), BF16),
            pltpu.VMEM((F, S_BLK, wid), BF16),
            pltpu.VMEM((2, S_BLK, wid), BF16),
            pltpu.VMEM((near, 2, S_BLK, wid), BF16),
            pltpu.VMEM((F, S_BLK, wid), BF16),
            pltpu.VMEM((H * S_BLK, wid), BF16),
            pltpu.VMEM((H * S_BLK, S_BLK), F32),
            pltpu.VMEM((H * S_BLK, wid), F32),
            dma((rows // CHUNK + 3,)),
            dma((F,)), dma((F,)),
            dma((T, R)), dma((T, R)),
            dma((T,)), dma((T,)),
            dma((T,)), dma((T,)),
            dma((F,)), dma((F,)),
            dma((near, 2)), dma((near, 2)),
            dma((F,)), dma((F,)),
        ],
        compiler_params=pltpu.CompilerParams(
            collective_id=0, has_side_effects=True, vmem_limit_bytes=48 * 1024 * 1024
        ),
    )(
        dest_tile.reshape(1, rows), member.reshape(1, rows), temper, adjacency,
        ln_gain.reshape(1, dim), points, w_point, w_qkv, w_out,
    )


def solution(mesh):
    return jax.shard_map(
        body,
        mesh=mesh,
        in_specs=(
            P(("groups", "tiles", "rep"), None),
            P(("groups", "tiles", "rep"), None),
            P(("groups", "tiles", "rep")),
            P(None, "feat"),
            P(),
            P(None, None, "feat"),
            P("feat"),
            P("feat", None),
            P(("groups", "tiles", "rep"), None),
        ),
        out_specs=P(("groups", "tiles", "rep"), "feat"),
        check_vma=False,
    )
```

```python
import functools

import jax
import jax.numpy as jnp
from jax import lax
from jax.experimental import pallas as pl
from jax.experimental.pallas import tpu as pltpu
from jax.sharding import PartitionSpec as P

S_BLK = 128
REACH = 2
HEAD = 64
CHUNK = 1024
MESH = pl.DeviceIdType.MESH
OFFSETS = tuple(range(-REACH, 0)) + tuple(range(1, REACH + 1))
NT = (((1,), (1,)), ((), ()))
F32 = jnp.float32
BF16 = jnp.bfloat16


def loop(count, step):
    if count <= 8:
        for k in range(count):
            step(k)
    else:
        lax.fori_loop(0, count, lambda k, c: (step(k), c)[1], 0)


def kernel(
    T, R, F, H,
    dest_hbm, member_hbm, temper_hbm, adj_hbm, gain_hbm, points_hbm, wp_hbm, wqkv_hbm, wo_hbm,
    out_ref,
    dest_ref, member_ref, temper_ref, adj_ref, gain_ref, pts, wp, wqkv, wo, hid, moh, cnt_send, cnt_recv, tsum, rep_send, rep_recv, z_send, z_recv,
    pool, kv_own, kv_recv, att, qm, lsum, acc,
    in_sem, wo_ss, wo_rs, cnt_ss, cnt_rs, rep_ss, rep_rs, z_ss, z_rs, pool_ss, pool_rs,
    kv_ss, kv_rs, att_ss, att_rs,
):
    t, r, f = lax.axis_index("tiles"), lax.axis_index("rep"), lax.axis_index("feat")
    other = 1 - r
    rows = pts.shape[0]
    dim = pts.shape[1]
    wid = wp.shape[1]
    chunks = rows // CHUNK
    blocks = T * R
    block = t * R + r

    loads = [pltpu.make_async_copy(wp_hbm, wp, in_sem.at[chunks])]
    for c in range(chunks):
        part = pl.ds(c * CHUNK, CHUNK)
        loads.append(pltpu.make_async_copy(points_hbm.at[part], pts.at[part], in_sem.at[c]))
    loads.append(pltpu.make_async_copy(wqkv_hbm, wqkv, in_sem.at[chunks + 1]))
    my_cols = pl.ds(pl.multiple_of(f * wid, 128), wid)
    loads.append(pltpu.make_async_copy(wo_hbm.at[:, my_cols], wo.at[f], in_sem.at[chunks + 2]))
    ids_in = [
        pltpu.make_async_copy(member_hbm, member_ref, in_sem.at[chunks + 3]),
        pltpu.make_async_copy(dest_hbm, dest_ref, in_sem.at[chunks + 4]),
    ]
    small = [
        pltpu.make_async_copy(temper_hbm, temper_ref, in_sem.at[chunks + 5]),
        pltpu.make_async_copy(adj_hbm, adj_ref, in_sem.at[chunks + 6]),
        pltpu.make_async_copy(gain_hbm, gain_ref, in_sem.at[chunks + 7]),
    ]
    for load in ids_in + loads + small:
        load.start()

    barrier = pltpu.get_barrier_semaphore()

    def greet(i):
        pl.semaphore_signal(
            barrier, inc=1, device_id={"tiles": lax.rem(t + i, T), "rep": r}, device_id_type=MESH
        )
        pl.semaphore_signal(
            barrier, inc=1, device_id={"tiles": lax.rem(t + i, T), "rep": other},
            device_id_type=MESH,
        )

    loop(T - 1, lambda k: greet(k + 1))
    pl.semaphore_signal(barrier, inc=1, device_id={"rep": other}, device_id_type=MESH)
    for i in range(1, F):
        pl.semaphore_signal(
            barrier, inc=1, device_id={"feat": lax.rem(f + i, F)}, device_id_type=MESH
        )

    for load in ids_in:
        load.wait()

    t_rows = max(T, 16)
    counts = jnp.zeros((t_rows, R * S_BLK), F32)
    for c in range(chunks):
        cols = pl.ds(c * CHUNK, CHUNK)
        ids = lax.broadcasted_iota(jnp.int32, (R * S_BLK, CHUNK), 0)
        hot = jnp.where(ids == member_ref[:, cols], 1.0, 0.0).astype(BF16)
        moh[:, cols] = hot
        tids = lax.broadcasted_iota(jnp.int32, (t_rows, CHUNK), 0)
        thot = jnp.where(tids == dest_ref[:, cols], 1.0, 0.0).astype(BF16)
        counts += lax.dot_general(thot, hot, NT, preferred_element_type=F32)
    for i in range(T):
        for j in range(R):
            cnt_send[i, j] = jnp.broadcast_to(
                counts[i : i + 1, j * S_BLK : (j + 1) * S_BLK], (8, S_BLK)
            )

    pl.semaphore_wait(barrier, R * T - 1 + F - 1)

    def remote(src, dst, ss, rs, device):
        return pltpu.make_async_remote_copy(
            src_ref=src, dst_ref=dst, send_sem=ss, recv_sem=rs, device_id=device,
            device_id_type=MESH,
        )

    def wo_copy(i):
        p = lax.rem(f + i, F)
        cols = pl.ds(pl.multiple_of(p * wid, 128), wid)
        return remote(wo_hbm.at[:, cols], wo.at[f], wo_ss.at[p], wo_rs.at[f], {"feat": p})

    def cnt_copy(i, j):
        p = lax.rem(t + i, T)
        return remote(
            cnt_send.at[p, j], cnt_recv.at[t, r], cnt_ss.at[p, j], cnt_rs.at[t, r],
            {"tiles": p, "rep": j},
        )

    loop(T - 1, lambda k: (cnt_copy(k + 1, r).start(), cnt_copy(k + 1, other).start()))
    cnt_copy(0, other).start()
    for i in range(1, F):
        wo_copy(i).start()

    loads[0].wait()
    for c in range(chunks):
        loads[1 + c].wait()
        part = pl.ds(c * CHUNK, CHUNK)
        x = jnp.dot(pts[part], wp[...], preferred_element_type=F32)
        inner = 0.7978845608028654 * (x + 0.044715 * (x * x * x))
        hid[part] = (0.5 * x * (1.0 + jnp.tanh(inner))).astype(BF16)

    def tile_at(k):
        return lax.rem(t + 1 + lax.rem(T // 2 - 1 - k + (T - 1), T - 1), T)

    def rep_copy(k):
        return remote(
            rep_send.at[k], rep_recv.at[k], rep_ss.at[k], rep_rs.at[k], {"rep": other}
        )

    def z_copy(k):
        return remote(
            z_send.at[k], z_recv.at[t], z_ss.at[k], z_rs.at[t], {"tiles": tile_at(k)}
        )

    def sum_tile(k, tile):
        here = jnp.where(dest_ref[...] == tile, 1.0, 0.0).astype(BF16)
        sums = jnp.dot(moh[...] * here, hid[...], preferred_element_type=F32)
        for j in range(R):
            tsum[k, j] = sums[j * S_BLK : (j + 1) * S_BLK]
        rep_send[k] = tsum[k, other].astype(BF16)
        rep_copy(k).start()

    def pass_on(k):
        rep_copy(k).wait_recv()
        z_send[k] = (tsum[k, r] + rep_recv[k].astype(F32)).astype(BF16)
        z_copy(k).start()

    sum_tile(0, tile_at(0))

    def middle(k):
        sum_tile(k + 1, tile_at(k + 1))
        pass_on(k)

    loop(T - 2, middle)
    sum_tile(T - 1, t)
    pass_on(T - 2)

    cnt_recv[t, r] = cnt_send[t, r]

    def cnt_wait(i, j):
        p = lax.rem(t + i, T)
        remote(
            cnt_send.at[p, j], cnt_recv.at[p, j], cnt_ss.at[p, j], cnt_rs.at[p, j],
            {"tiles": p, "rep": j},
        ).wait_recv()

    loop(T - 1, lambda k: (cnt_wait(k + 1, r), cnt_wait(k + 1, other)))
    cnt_wait(0, other)
    total = jnp.sum(cnt_recv[...].reshape(blocks, 8, S_BLK), axis=0)
    column = jnp.transpose(jnp.broadcast_to(total[0:1], (S_BLK, S_BLK)))
    column = jnp.maximum(column, 1.0)

    rep_copy(T - 1).wait_recv()
    tsum[T - 1, r] += rep_recv[T - 1].astype(F32)

    def gather_sum(i):
        p = lax.rem(t + i, T)
        remote(z_send.at[0], z_recv.at[p], z_ss.at[0], z_rs.at[p], {"tiles": p}).wait_recv()
        tsum[T - 1, r] += z_recv[p].astype(F32)

    loop(T - 1, lambda k: gather_sum(k + 1))
    sums = tsum[T - 1, r]
    pooled = jnp.concatenate(
        [sums[:, g * 128 : (g + 1) * 128] / column for g in range(wid // 128)], axis=1
    ).astype(BF16)
    pool[f] = pooled

    def feat_copy(ref, ss, rs, i):
        p = lax.rem(f + i, F)
        return remote(ref.at[f], ref.at[f], ss.at[p], rs.at[f], {"feat": p})

    def feat_wait(ref, ss, rs, i):
        p = lax.rem(f + i, F)
        remote(ref.at[p], ref.at[p], ss.at[p], rs.at[p], {"feat": p}).wait_recv()

    for i in range(1, F):
        feat_copy(pool, pool_ss, pool_rs, i).start()
    loads[chunks + 1].wait()
    for load in small:
        load.wait()
    for i in range(1, F):
        feat_wait(pool, pool_ss, pool_rs, i)

    lifted = jnp.concatenate([pool[p].astype(F32) for p in range(F)], axis=1)
    mean = jnp.sum(lifted, axis=1, keepdims=True) * (1.0 / dim)
    centred = lifted - mean
    var = jnp.sum(centred * centred, axis=1, keepdims=True) * (1.0 / dim)
    normed = (centred * lax.rsqrt(var + 1e-05) * gain_ref[...]).astype(BF16)

    same_head = (
        lax.broadcasted_iota(jnp.int32, (wid, wid), 0) // HEAD
        == lax.broadcasted_iota(jnp.int32, (wid, wid), 1) // HEAD
    )
    spread = jnp.where(same_head, 1.0, 0.0).astype(BF16)

    def project(i):
        return jnp.dot(normed, wqkv[i], preferred_element_type=F32)

    def unit(proj):
        square = proj * proj
        high = square.astype(BF16)
        low = (square - high.astype(F32)).astype(BF16)
        norm = jnp.dot(high, spread, preferred_element_type=F32) + jnp.dot(
            low, spread, preferred_element_type=F32
        )
        return (proj * lax.rsqrt(norm + 1e-06)).astype(BF16)

    def inside(offset):
        return (block + offset >= 0) & (block + offset < blocks)

    def kv_copy(i, j):
        slot = len(OFFSETS) - 1 - j
        goal = block + OFFSETS[j]
        return remote(
            kv_own.at[i], kv_recv.at[slot, i], kv_ss.at[j, i], kv_rs.at[slot, i],
            {"tiles": goal // R, "rep": lax.rem(goal, R)},
        )

    def kv_wait(i, j):
        goal = block + OFFSETS[j]
        remote(
            kv_own.at[i], kv_recv.at[j, i], kv_ss.at[j, i], kv_rs.at[j, i],
            {"tiles": goal // R, "rep": lax.rem(goal, R)},
        ).wait_recv()

    def send_kv(i):
        for j in (0, len(OFFSETS) - 1, 1, 2):
            @pl.when(inside(OFFSETS[j]))
            def _():
                kv_copy(i, j).start()

    kv_own[0] = unit(project(1))
    send_kv(0)
    kv_own[1] = project(2).astype(BF16)
    send_kv(1)
    query = unit(project(0))
    temper = temper_ref[...]
    lane_head = lax.broadcasted_iota(jnp.int32, (S_BLK, wid), 1) // HEAD
    for h in range(H):
        qm[h * S_BLK : (h + 1) * S_BLK] = jnp.where(lane_head == h, query, jnp.zeros_like(query))

    def attend(keys, values, mask, first):
        scores = lax.dot_general(qm[...], keys, NT, preferred_element_type=F32)
        expd = jnp.concatenate(
            [
                jnp.exp(scores[h * S_BLK : (h + 1) * S_BLK] * temper[:, h : h + 1])
                for h in range(H)
            ],
            axis=0,
        )
        if mask is not None:
            expd = expd * mask
        got = jnp.dot(expd.astype(BF16), values, preferred_element_type=F32)
        if first:
            lsum[...] = expd
            acc[...] = got
        else:
            lsum[...] += expd
            acc[...] += got

    attend(kv_own[0], kv_own[1], None, True)
    for j in (1, 2, 0, 3):
        @pl.when(inside(OFFSETS[j]))
        def _():
            kv_wait(0, j)
            kv_wait(1, j)
            mask = jnp.where(adj_ref[:, j : j + 1] == 1, 1.0, 0.0).astype(F32)
            attend(kv_recv[j, 0], kv_recv[j, 1], mask, False)

    attended = jnp.zeros((S_BLK, wid), F32)
    for h in range(H):
        part = slice(h * S_BLK, (h + 1) * S_BLK)
        scale = 1.0 / jnp.sum(lsum[part], axis=1, keepdims=True)
        attended = jnp.where(lane_head == h, acc[part] * scale, attended)
    att[f] = attended.astype(BF16)
    for i in range(1, F):
        feat_copy(att, att_ss, att_rs, i).start()
    loads[chunks + 2].wait()
    mixed = pool[f].astype(F32) + jnp.dot(att[f], wo[f], preferred_element_type=F32)
    for i in range(1, F):
        p = lax.rem(f + i, F)
        remote(wo.at[p], wo.at[p], wo_ss.at[p], wo_rs.at[p], {"feat": p}).wait_recv()
        feat_wait(att, att_ss, att_rs, i)
        mixed += jnp.dot(att[p], wo[p], preferred_element_type=F32)
    out_ref[...] = mixed.astype(out_ref.dtype)

    loop(T - 1, lambda k: (cnt_copy(k + 1, r).wait_send(), cnt_copy(k + 1, other).wait_send()))
    cnt_copy(0, other).wait_send()
    loop(T, lambda k: rep_copy(k).wait_send())
    loop(T - 1, lambda k: z_copy(k).wait_send())
    for i in range(1, F):
        wo_copy(i).wait_send()
        feat_copy(pool, pool_ss, pool_rs, i).wait_send()
        feat_copy(att, att_ss, att_rs, i).wait_send()
    for j in range(len(OFFSETS)):
        @pl.when(inside(OFFSETS[j]))
        def _():
            kv_copy(0, j).wait_send()
            kv_copy(1, j).wait_send()


def body(points, dest_tile, member, w_point, ln_gain, w_qkv, temper, w_out, adjacency):
    T, R, F = lax.axis_size("tiles"), lax.axis_size("rep"), lax.axis_size("feat")
    H = temper.shape[0]
    rows, dim = points.shape
    wid = w_point.shape[1]
    near = len(OFFSETS)
    vmem = pl.BlockSpec(memory_space=pltpu.VMEM)
    hbm = pl.BlockSpec(memory_space=pl.ANY)
    dma = pltpu.SemaphoreType.DMA
    return pl.pallas_call(
        functools.partial(kernel, T, R, F, H),
        out_shape=jax.ShapeDtypeStruct((S_BLK, wid), BF16),
        in_specs=[hbm] * 9,
        out_specs=vmem,
        scratch_shapes=[
            pltpu.VMEM((1, rows), jnp.int32),
            pltpu.VMEM((1, rows), jnp.int32),
            pltpu.VMEM((1, H), F32),
            pltpu.VMEM(adjacency.shape, jnp.int32),
            pltpu.VMEM((1, dim), F32),
            pltpu.VMEM((rows, dim), BF16),
            pltpu.VMEM((dim, wid), BF16),
            pltpu.VMEM((3, dim, wid), BF16),
            pltpu.VMEM((F, wid, wid), BF16),
            pltpu.VMEM((rows, wid), BF16),
            pltpu.VMEM((R * S_BLK, rows), BF16),
            pltpu.VMEM((T, R, 8, S_BLK), F32),
            pltpu.VMEM((T, R, 8, S_BLK), F32),
            pltpu.VMEM((T, R, S_BLK, wid), F32),
            pltpu.VMEM((T, S_BLK, wid), BF16),
            pltpu.VMEM((T, S_BLK, wid), BF16),
            pltpu.VMEM((T, S_BLK, wid), BF16),
            pltpu.VMEM((T, S_BLK, wid), BF16),
            pltpu.VMEM((F, S_BLK, wid), BF16),
            pltpu.VMEM((2, S_BLK, wid), BF16),
            pltpu.VMEM((near, 2, S_BLK, wid), BF16),
            pltpu.VMEM((F, S_BLK, wid), BF16),
            pltpu.VMEM((H * S_BLK, wid), BF16),
            pltpu.VMEM((H * S_BLK, S_BLK), F32),
            pltpu.VMEM((H * S_BLK, wid), F32),
            dma((rows // CHUNK + 8,)),
            dma((F,)), dma((F,)),
            dma((T, R)), dma((T, R)),
            dma((T,)), dma((T,)),
            dma((T,)), dma((T,)),
            dma((F,)), dma((F,)),
            dma((near, 2)), dma((near, 2)),
            dma((F,)), dma((F,)),
        ],
        compiler_params=pltpu.CompilerParams(
            collective_id=0, has_side_effects=True, vmem_limit_bytes=56000 * 1024
        ),
    )(
        dest_tile.reshape(1, rows), member.reshape(1, rows), temper.reshape(1, H), adjacency,
        ln_gain.reshape(1, dim), points, w_point, w_qkv, w_out,
    )


def solution(mesh):
    return jax.shard_map(
        body,
        mesh=mesh,
        in_specs=(
            P(("groups", "tiles", "rep"), None),
            P(("groups", "tiles", "rep"), None),
            P(("groups", "tiles", "rep")),
            P(None, "feat"),
            P(),
            P(None, None, "feat"),
            P("feat"),
            P("feat", None),
            P(("groups", "tiles", "rep"), None),
        ),
        out_specs=P(("groups", "tiles", "rep"), "feat"),
        check_vma=False,
    )
```

```python
import functools

import jax
import jax.numpy as jnp
from jax import lax
from jax.experimental import pallas as pl
from jax.experimental.pallas import tpu as pltpu
from jax.sharding import PartitionSpec as P

S_BLK = 128
REACH = 2
HEAD = 64
CHUNK = 1024
MESH = pl.DeviceIdType.MESH
OFFSETS = tuple(range(-REACH, 0)) + tuple(range(1, REACH + 1))
NT = (((1,), (1,)), ((), ()))
F32 = jnp.float32
BF16 = jnp.bfloat16


def loop(count, step):
    if count <= 8:
        for k in range(count):
            step(k)
    else:
        lax.fori_loop(0, count, lambda k, c: (step(k), c)[1], 0)


def kernel(
    T, R, F, H,
    dest_hbm, member_hbm, temper_hbm, adj_hbm, gain_hbm, points_hbm, wp_hbm, wqkv_hbm, wo_hbm,
    out_ref,
    dest_ref, member_ref, temper_ref, adj_ref, gain_ref, pts, wp, wqkv, wo, hid, moh, cnt_send, cnt_recv, tsum, rep_send, rep_recv, z_send, z_recv,
    pool, kv_own, kv_recv, att, qm, lsum, acc,
    in_sem, wo_ss, wo_rs, cnt_ss, cnt_rs, rep_ss, rep_rs, z_ss, z_rs, pool_ss, pool_rs,
    kv_ss, kv_rs, att_ss, att_rs,
):
    t, r, f = lax.axis_index("tiles"), lax.axis_index("rep"), lax.axis_index("feat")
    other = 1 - r
    rows = pts.shape[0]
    dim = pts.shape[1]
    wid = wp.shape[1]
    chunks = rows // CHUNK
    blocks = T * R
    block = t * R + r

    loads = [pltpu.make_async_copy(wp_hbm, wp, in_sem.at[chunks])]
    for c in range(chunks):
        part = pl.ds(c * CHUNK, CHUNK)
        loads.append(pltpu.make_async_copy(points_hbm.at[part], pts.at[part], in_sem.at[c]))
    loads.append(pltpu.make_async_copy(wqkv_hbm, wqkv, in_sem.at[chunks + 1]))
    my_cols = pl.ds(pl.multiple_of(f * wid, 128), wid)
    loads.append(pltpu.make_async_copy(wo_hbm.at[:, my_cols], wo.at[f], in_sem.at[chunks + 2]))
    ids_in = [
        pltpu.make_async_copy(member_hbm, member_ref, in_sem.at[chunks + 3]),
        pltpu.make_async_copy(dest_hbm, dest_ref, in_sem.at[chunks + 4]),
    ]
    small = [
        pltpu.make_async_copy(temper_hbm, temper_ref, in_sem.at[chunks + 5]),
        pltpu.make_async_copy(adj_hbm, adj_ref, in_sem.at[chunks + 6]),
        pltpu.make_async_copy(gain_hbm, gain_ref, in_sem.at[chunks + 7]),
    ]
    for load in ids_in + loads + small:
        load.start()

    barrier = pltpu.get_barrier_semaphore()

    def greet(i):
        pl.semaphore_signal(
            barrier, inc=1, device_id={"tiles": lax.rem(t + i, T), "rep": r}, device_id_type=MESH
        )
        pl.semaphore_signal(
            barrier, inc=1, device_id={"tiles": lax.rem(t + i, T), "rep": other},
            device_id_type=MESH,
        )

    loop(T - 1, lambda k: greet(k + 1))
    pl.semaphore_signal(barrier, inc=1, device_id={"rep": other}, device_id_type=MESH)
    for i in range(1, F):
        pl.semaphore_signal(
            barrier, inc=1, device_id={"feat": lax.rem(f + i, F)}, device_id_type=MESH
        )

    for load in ids_in:
        load.wait()

    t_rows = max(T, 16)
    counts = jnp.zeros((t_rows, R * S_BLK), F32)
    for c in range(chunks):
        cols = pl.ds(c * CHUNK, CHUNK)
        ids = lax.broadcasted_iota(jnp.int32, (R * S_BLK, CHUNK), 0)
        hot = jnp.where(ids == member_ref[:, cols], 1.0, 0.0).astype(BF16)
        moh[:, cols] = hot
        tids = lax.broadcasted_iota(jnp.int32, (t_rows, CHUNK), 0)
        thot = jnp.where(tids == dest_ref[:, cols], 1.0, 0.0).astype(BF16)
        counts += lax.dot_general(thot, hot, NT, preferred_element_type=F32)
    for i in range(T):
        for j in range(R):
            cnt_send[i, j] = jnp.broadcast_to(
                counts[i : i + 1, j * S_BLK : (j + 1) * S_BLK], (8, S_BLK)
            )

    pl.semaphore_wait(barrier, R * T - 1 + F - 1)

    def remote(src, dst, ss, rs, device):
        return pltpu.make_async_remote_copy(
            src_ref=src, dst_ref=dst, send_sem=ss, recv_sem=rs, device_id=device,
            device_id_type=MESH,
        )

    def wo_copy(i):
        p = lax.rem(f + i, F)
        cols = pl.ds(pl.multiple_of(p * wid, 128), wid)
        return remote(wo_hbm.at[:, cols], wo.at[f], wo_ss.at[p], wo_rs.at[f], {"feat": p})

    def cnt_copy(i, j):
        p = lax.rem(t + i, T)
        return remote(
            cnt_send.at[p, j], cnt_recv.at[t, r], cnt_ss.at[p, j], cnt_rs.at[t, r],
            {"tiles": p, "rep": j},
        )

    loop(T - 1, lambda k: (cnt_copy(k + 1, r).start(), cnt_copy(k + 1, other).start()))
    cnt_copy(0, other).start()
    for i in range(1, F):
        wo_copy(i).start()

    loads[0].wait()
    for c in range(chunks):
        loads[1 + c].wait()
        part = pl.ds(c * CHUNK, CHUNK)
        x = jnp.dot(pts[part], wp[...], preferred_element_type=F32)
        inner = 0.7978845608028654 * (x + 0.044715 * (x * x * x))
        hid[part] = (0.5 * x * (1.0 + jnp.tanh(inner))).astype(BF16)

    def tile_at(k):
        return lax.rem(t + 1 + lax.rem(T // 2 - 1 - k + (T - 1), T - 1), T)

    def rep_copy(k):
        return remote(
            rep_send.at[k], rep_recv.at[k], rep_ss.at[k], rep_rs.at[k], {"rep": other}
        )

    def z_copy(k):
        return remote(
            z_send.at[k], z_recv.at[t], z_ss.at[k], z_rs.at[t], {"tiles": tile_at(k)}
        )

    def sum_tile(k, tile):
        here = jnp.where(dest_ref[...] == tile, 1.0, 0.0).astype(BF16)
        sums = jnp.dot(moh[...] * here, hid[...], preferred_element_type=F32)
        for j in range(R):
            tsum[k, j] = sums[j * S_BLK : (j + 1) * S_BLK]
        rep_send[k] = tsum[k, other].astype(BF16)
        rep_copy(k).start()

    def pass_on(k):
        rep_copy(k).wait_recv()
        z_send[k] = (tsum[k, r] + rep_recv[k].astype(F32)).astype(BF16)
        z_copy(k).start()

    sum_tile(0, tile_at(0))

    def middle(k):
        sum_tile(k + 1, tile_at(k + 1))
        pass_on(k)

    loop(T - 2, middle)
    sum_tile(T - 1, t)
    pass_on(T - 2)

    cnt_recv[t, r] = cnt_send[t, r]

    def cnt_wait(i, j):
        p = lax.rem(t + i, T)
        remote(
            cnt_send.at[p, j], cnt_recv.at[p, j], cnt_ss.at[p, j], cnt_rs.at[p, j],
            {"tiles": p, "rep": j},
        ).wait_recv()

    loop(T - 1, lambda k: (cnt_wait(k + 1, r), cnt_wait(k + 1, other)))
    cnt_wait(0, other)
    total = jnp.sum(cnt_recv[...].reshape(blocks, 8, S_BLK), axis=0)
    column = jnp.transpose(jnp.broadcast_to(total[0:1], (S_BLK, S_BLK)))
    column = jnp.maximum(column, 1.0)

    rep_copy(T - 1).wait_recv()
    tsum[T - 1, r] += rep_recv[T - 1].astype(F32)

    def gather_sum(i):
        p = lax.rem(t + i, T)
        remote(z_send.at[0], z_recv.at[p], z_ss.at[0], z_rs.at[p], {"tiles": p}).wait_recv()
        tsum[T - 1, r] += z_recv[p].astype(F32)

    loop(T - 1, lambda k: gather_sum(k + 1))
    sums = tsum[T - 1, r]
    pooled = jnp.concatenate(
        [sums[:, g * 128 : (g + 1) * 128] / column for g in range(wid // 128)], axis=1
    ).astype(BF16)
    pool[f] = pooled

    def feat_copy(ref, ss, rs, i):
        p = lax.rem(f + i, F)
        return remote(ref.at[f], ref.at[f], ss.at[p], rs.at[f], {"feat": p})

    def feat_wait(ref, ss, rs, i):
        p = lax.rem(f + i, F)
        remote(ref.at[p], ref.at[p], ss.at[p], rs.at[p], {"feat": p}).wait_recv()

    for i in range(1, F):
        feat_copy(pool, pool_ss, pool_rs, i).start()
    loads[chunks + 1].wait()
    for load in small:
        load.wait()
    for i in range(1, F):
        feat_wait(pool, pool_ss, pool_rs, i)

    lifted = jnp.concatenate([pool[p].astype(F32) for p in range(F)], axis=1)
    mean = jnp.sum(lifted, axis=1, keepdims=True) * (1.0 / dim)
    centred = lifted - mean
    var = jnp.sum(centred * centred, axis=1, keepdims=True) * (1.0 / dim)
    normed = (centred * lax.rsqrt(var + 1e-05) * gain_ref[...]).astype(BF16)

    same_head = (
        lax.broadcasted_iota(jnp.int32, (wid, wid), 0) // HEAD
        == lax.broadcasted_iota(jnp.int32, (wid, wid), 1) // HEAD
    )
    spread = jnp.where(same_head, 1.0, 0.0).astype(BF16)

    def project(i):
        return jnp.dot(normed, wqkv[i], preferred_element_type=F32)

    def unit(proj):
        square = proj * proj
        high = square.astype(BF16)
        low = (square - high.astype(F32)).astype(BF16)
        norm = jnp.dot(high, spread, preferred_element_type=F32) + jnp.dot(
            low, spread, preferred_element_type=F32
        )
        return (proj * lax.rsqrt(norm + 1e-06)).astype(BF16)

    def inside(offset):
        return (block + offset >= 0) & (block + offset < blocks)

    sib, cross, handed = 2 - r, 1 + r, 3 * (1 - r)
    steps = {0: -1, 3: 1}

    def kv_copy(i, j):
        slot = len(OFFSETS) - 1 - j
        return remote(
            kv_own.at[i], kv_recv.at[slot, i], kv_ss.at[j, i], kv_rs.at[slot, i],
            {"tiles": t + steps[j]},
        )

    def sib_copy(i):
        return remote(
            kv_own.at[i], kv_recv.at[1 + r, i], kv_ss.at[sib, i], kv_rs.at[1 + r, i],
            {"rep": other},
        )

    def hand_copy(i):
        return remote(
            kv_recv.at[handed, i], kv_recv.at[2 - r, i], kv_ss.at[cross, i],
            kv_rs.at[2 - r, i], {"rep": other},
        )

    def kv_wait(i, j):
        remote(
            kv_own.at[i], kv_recv.at[j, i], kv_ss.at[j, i], kv_rs.at[j, i], {"rep": other}
        ).wait_recv()

    def send_kv(i):
        for j in steps:
            @pl.when(inside(OFFSETS[j]))
            def _():
                kv_copy(i, j).start()
        sib_copy(i).start()

    kv_own[0] = unit(project(1))
    send_kv(0)
    kv_own[1] = project(2).astype(BF16)
    send_kv(1)
    query = unit(project(0))
    temper = temper_ref[...]
    lane_head = lax.broadcasted_iota(jnp.int32, (S_BLK, wid), 1) // HEAD
    for h in range(H):
        qm[h * S_BLK : (h + 1) * S_BLK] = jnp.where(lane_head == h, query, jnp.zeros_like(query))

    def attend(keys, values, mask, first):
        scores = lax.dot_general(qm[...], keys, NT, preferred_element_type=F32)
        expd = jnp.concatenate(
            [
                jnp.exp(scores[h * S_BLK : (h + 1) * S_BLK] * temper[:, h : h + 1])
                for h in range(H)
            ],
            axis=0,
        )
        if mask is not None:
            expd = expd * mask
        got = jnp.dot(expd.astype(BF16), values, preferred_element_type=F32)
        if first:
            lsum[...] = expd
            acc[...] = got
        else:
            lsum[...] += expd
            acc[...] += got

    attend(kv_own[0], kv_own[1], None, True)

    def take(j):
        lanes = lax.broadcasted_iota(jnp.int32, adj_ref.shape, 1)
        on = jnp.where((lanes == j) & (adj_ref[...] == 1), 1.0, 0.0)
        mask = jnp.sum(on, axis=1, keepdims=True)
        attend(kv_recv[j, 0], kv_recv[j, 1], mask, False)

    kv_wait(0, sib)
    kv_wait(1, sib)
    take(sib)

    @pl.when(inside(2 - 4 * r))
    def _():
        for i in range(2):
            kv_wait(i, handed)
            hand_copy(i).start()
        take(handed)

    @pl.when(inside(4 * r - 2))
    def _():
        kv_wait(0, 3 - handed)
        kv_wait(1, 3 - handed)
        take(3 - handed)

    @pl.when(inside(2 * r - 1))
    def _():
        kv_wait(0, cross)
        kv_wait(1, cross)
        take(cross)

    attended = jnp.zeros((S_BLK, wid), F32)
    for h in range(H):
        part = slice(h * S_BLK, (h + 1) * S_BLK)
        scale = 1.0 / jnp.sum(lsum[part], axis=1, keepdims=True)
        attended = jnp.where(lane_head == h, acc[part] * scale, attended)
    att[f] = attended.astype(BF16)
    for i in range(1, F):
        feat_copy(att, att_ss, att_rs, i).start()
    loads[chunks + 2].wait()
    mixed = pool[f].astype(F32) + jnp.dot(att[f], wo[f], preferred_element_type=F32)
    for i in range(1, F):
        p = lax.rem(f + i, F)
        remote(wo.at[p], wo.at[p], wo_ss.at[p], wo_rs.at[p], {"feat": p}).wait_recv()
        feat_wait(att, att_ss, att_rs, i)
        mixed += jnp.dot(att[p], wo[p], preferred_element_type=F32)
    out_ref[...] = mixed.astype(out_ref.dtype)

    loop(T - 1, lambda k: (cnt_copy(k + 1, r).wait_send(), cnt_copy(k + 1, other).wait_send()))
    cnt_copy(0, other).wait_send()
    loop(T, lambda k: rep_copy(k).wait_send())
    loop(T - 1, lambda k: z_copy(k).wait_send())
    for i in range(1, F):
        wo_copy(i).wait_send()
        feat_copy(pool, pool_ss, pool_rs, i).wait_send()
        feat_copy(att, att_ss, att_rs, i).wait_send()
    for i in range(2):
        sib_copy(i).wait_send()
    for j in steps:
        @pl.when(inside(OFFSETS[j]))
        def _():
            kv_copy(0, j).wait_send()
            kv_copy(1, j).wait_send()

    @pl.when(inside(2 - 4 * r))
    def _():
        hand_copy(0).wait_send()
        hand_copy(1).wait_send()


def body(points, dest_tile, member, w_point, ln_gain, w_qkv, temper, w_out, adjacency):
    T, R, F = lax.axis_size("tiles"), lax.axis_size("rep"), lax.axis_size("feat")
    H = temper.shape[0]
    rows, dim = points.shape
    wid = w_point.shape[1]
    near = len(OFFSETS)
    vmem = pl.BlockSpec(memory_space=pltpu.VMEM)
    hbm = pl.BlockSpec(memory_space=pl.ANY)
    dma = pltpu.SemaphoreType.DMA
    return pl.pallas_call(
        functools.partial(kernel, T, R, F, H),
        out_shape=jax.ShapeDtypeStruct((S_BLK, wid), BF16),
        in_specs=[hbm] * 9,
        out_specs=vmem,
        scratch_shapes=[
            pltpu.VMEM((1, rows), jnp.int32),
            pltpu.VMEM((1, rows), jnp.int32),
            pltpu.VMEM((1, H), F32),
            pltpu.VMEM(adjacency.shape, jnp.int32),
            pltpu.VMEM((1, dim), F32),
            pltpu.VMEM((rows, dim), BF16),
            pltpu.VMEM((dim, wid), BF16),
            pltpu.VMEM((3, dim, wid), BF16),
            pltpu.VMEM((F, wid, wid), BF16),
            pltpu.VMEM((rows, wid), BF16),
            pltpu.VMEM((R * S_BLK, rows), BF16),
            pltpu.VMEM((T, R, 8, S_BLK), F32),
            pltpu.VMEM((T, R, 8, S_BLK), F32),
            pltpu.VMEM((T, R, S_BLK, wid), F32),
            pltpu.VMEM((T, S_BLK, wid), BF16),
            pltpu.VMEM((T, S_BLK, wid), BF16),
            pltpu.VMEM((T, S_BLK, wid), BF16),
            pltpu.VMEM((T, S_BLK, wid), BF16),
            pltpu.VMEM((F, S_BLK, wid), BF16),
            pltpu.VMEM((2, S_BLK, wid), BF16),
            pltpu.VMEM((near, 2, S_BLK, wid), BF16),
            pltpu.VMEM((F, S_BLK, wid), BF16),
            pltpu.VMEM((H * S_BLK, wid), BF16),
            pltpu.VMEM((H * S_BLK, S_BLK), F32),
            pltpu.VMEM((H * S_BLK, wid), F32),
            dma((rows // CHUNK + 8,)),
            dma((F,)), dma((F,)),
            dma((T, R)), dma((T, R)),
            dma((T,)), dma((T,)),
            dma((T,)), dma((T,)),
            dma((F,)), dma((F,)),
            dma((near, 2)), dma((near, 2)),
            dma((F,)), dma((F,)),
        ],
        compiler_params=pltpu.CompilerParams(
            collective_id=0, has_side_effects=True, vmem_limit_bytes=56000 * 1024
        ),
    )(
        dest_tile.reshape(1, rows), member.reshape(1, rows), temper.reshape(1, H), adjacency,
        ln_gain.reshape(1, dim), points, w_point, w_qkv, w_out,
    )


def solution(mesh):
    return jax.shard_map(
        body,
        mesh=mesh,
        in_specs=(
            P(("groups", "tiles", "rep"), None),
            P(("groups", "tiles", "rep"), None),
            P(("groups", "tiles", "rep")),
            P(None, "feat"),
            P(),
            P(None, None, "feat"),
            P("feat"),
            P("feat", None),
            P(("groups", "tiles", "rep"), None),
        ),
        out_specs=P(("groups", "tiles", "rep"), "feat"),
        check_vma=False,
    )
```

```python
import functools

import jax
import jax.numpy as jnp
from jax import lax
from jax.experimental import pallas as pl
from jax.experimental.pallas import tpu as pltpu
from jax.sharding import PartitionSpec as P

S_BLK = 128
REACH = 2
HEAD = 64
CHUNK = 2048
MESH = pl.DeviceIdType.MESH
OFFSETS = tuple(range(-REACH, 0)) + tuple(range(1, REACH + 1))
NT = (((1,), (1,)), ((), ()))
F32 = jnp.float32
BF16 = jnp.bfloat16


def loop(count, step):
    if count <= 8:
        for k in range(count):
            step(k)
    else:
        lax.fori_loop(0, count, lambda k, c: (step(k), c)[1], 0)


def kernel(
    T, R, F, H,
    dest_hbm, member_hbm, temper_hbm, adj_hbm, gain_hbm, points_hbm, wp_hbm, wqkv_hbm, wo_hbm,
    out_ref,
    dest_ref, member_ref, temper_ref, adj_ref, gain_ref, pts, wp, wqkv, wo, hid, moh, cnt_send, cnt_recv, tsum, rep_send, rep_recv, z_send, z_recv,
    pool, kv_own, kv_recv, att, qm, lsum, acc,
    in_sem, wo_ss, wo_rs, cnt_ss, cnt_rs, rep_ss, rep_rs, z_ss, z_rs, pool_ss, pool_rs,
    kv_ss, kv_rs, att_ss, att_rs,
):
    t, r, f = lax.axis_index("tiles"), lax.axis_index("rep"), lax.axis_index("feat")
    other = 1 - r
    rows = pts.shape[0]
    dim = pts.shape[1]
    wid = wp.shape[1]
    chunks = rows // CHUNK
    blocks = T * R
    block = t * R + r

    loads = [pltpu.make_async_copy(wp_hbm, wp, in_sem.at[chunks])]
    for c in range(chunks):
        part = pl.ds(c * CHUNK, CHUNK)
        loads.append(pltpu.make_async_copy(points_hbm.at[part], pts.at[part], in_sem.at[c]))
    loads.append(pltpu.make_async_copy(wqkv_hbm, wqkv, in_sem.at[chunks + 1]))
    my_cols = pl.ds(pl.multiple_of(f * wid, 128), wid)
    loads.append(pltpu.make_async_copy(wo_hbm.at[:, my_cols], wo.at[f], in_sem.at[chunks + 2]))
    ids_in = [
        pltpu.make_async_copy(member_hbm, member_ref, in_sem.at[chunks + 3]),
        pltpu.make_async_copy(dest_hbm, dest_ref, in_sem.at[chunks + 4]),
    ]
    small = [
        pltpu.make_async_copy(temper_hbm, temper_ref, in_sem.at[chunks + 5]),
        pltpu.make_async_copy(adj_hbm, adj_ref, in_sem.at[chunks + 6]),
        pltpu.make_async_copy(gain_hbm, gain_ref, in_sem.at[chunks + 7]),
    ]
    for load in ids_in + loads + small:
        load.start()

    barrier = pltpu.get_barrier_semaphore()

    def greet(i):
        pl.semaphore_signal(
            barrier, inc=1, device_id={"tiles": lax.rem(t + i, T), "rep": r}, device_id_type=MESH
        )
        pl.semaphore_signal(
            barrier, inc=1, device_id={"tiles": lax.rem(t + i, T), "rep": other},
            device_id_type=MESH,
        )

    loop(T - 1, lambda k: greet(k + 1))
    pl.semaphore_signal(barrier, inc=1, device_id={"rep": other}, device_id_type=MESH)
    for i in range(1, F):
        pl.semaphore_signal(
            barrier, inc=1, device_id={"feat": lax.rem(f + i, F)}, device_id_type=MESH
        )

    for load in ids_in:
        load.wait()

    t_rows = max(T, 16)
    counts = jnp.zeros((t_rows, R * S_BLK), F32)
    for c in range(chunks):
        cols = pl.ds(c * CHUNK, CHUNK)
        ids = lax.broadcasted_iota(jnp.int32, (R * S_BLK, CHUNK), 0)
        hot = jnp.where(ids == member_ref[:, cols], 1.0, 0.0).astype(BF16)
        moh[:, cols] = hot
        tids = lax.broadcasted_iota(jnp.int32, (t_rows, CHUNK), 0)
        thot = jnp.where(tids == dest_ref[:, cols], 1.0, 0.0).astype(BF16)
        counts += lax.dot_general(thot, hot, NT, preferred_element_type=F32)
    for i in range(T):
        for j in range(R):
            cnt_send[i, j] = jnp.broadcast_to(
                counts[i : i + 1, j * S_BLK : (j + 1) * S_BLK], (8, S_BLK)
            )

    pl.semaphore_wait(barrier, R * T - 1 + F - 1)

    def remote(src, dst, ss, rs, device):
        return pltpu.make_async_remote_copy(
            src_ref=src, dst_ref=dst, send_sem=ss, recv_sem=rs, device_id=device,
            device_id_type=MESH,
        )

    def wo_copy(i):
        p = lax.rem(f + i, F)
        cols = pl.ds(pl.multiple_of(p * wid, 128), wid)
        return remote(wo_hbm.at[:, cols], wo.at[f], wo_ss.at[p], wo_rs.at[f], {"feat": p})

    def cnt_copy(i, j):
        p = lax.rem(t + i, T)
        return remote(
            cnt_send.at[p, j], cnt_recv.at[t, r], cnt_ss.at[p, j], cnt_rs.at[t, r],
            {"tiles": p, "rep": j},
        )

    loop(T - 1, lambda k: (cnt_copy(k + 1, r).start(), cnt_copy(k + 1, other).start()))
    cnt_copy(0, other).start()
    for i in range(1, F):
        wo_copy(i).start()

    loads[0].wait()
    for c in range(chunks):
        loads[1 + c].wait()
        part = pl.ds(c * CHUNK, CHUNK)
        x = jnp.dot(pts[part], wp[...], preferred_element_type=F32)
        inner = 0.7978845608028654 * (x + 0.044715 * (x * x * x))
        hid[part] = (0.5 * x * (1.0 + jnp.tanh(inner))).astype(BF16)

    def tile_at(k):
        return lax.rem(t + 1 + lax.rem(T // 2 - 1 - k + (T - 1), T - 1), T)

    def rep_copy(k):
        return remote(
            rep_send.at[k], rep_recv.at[k], rep_ss.at[k], rep_rs.at[k], {"rep": other}
        )

    def z_copy(k):
        return remote(
            z_send.at[k], z_recv.at[t], z_ss.at[k], z_rs.at[t], {"tiles": tile_at(k)}
        )

    def sum_tile(k, tile):
        here = jnp.where(dest_ref[...] == tile, 1.0, 0.0).astype(BF16)
        sums = jnp.dot(moh[...] * here, hid[...], preferred_element_type=F32)
        for j in range(R):
            tsum[k, j] = sums[j * S_BLK : (j + 1) * S_BLK]
        rep_send[k] = tsum[k, other].astype(BF16)
        rep_copy(k).start()

    def pass_on(k):
        rep_copy(k).wait_recv()
        z_send[k] = (tsum[k, r] + rep_recv[k].astype(F32)).astype(BF16)
        z_copy(k).start()

    sum_tile(0, tile_at(0))

    def middle(k):
        sum_tile(k + 1, tile_at(k + 1))
        pass_on(k)

    loop(T - 2, middle)
    sum_tile(T - 1, t)
    pass_on(T - 2)

    cnt_recv[t, r] = cnt_send[t, r]

    def cnt_wait(i, j):
        p = lax.rem(t + i, T)
        remote(
            cnt_send.at[p, j], cnt_recv.at[p, j], cnt_ss.at[p, j], cnt_rs.at[p, j],
            {"tiles": p, "rep": j},
        ).wait_recv()

    loop(T - 1, lambda k: (cnt_wait(k + 1, r), cnt_wait(k + 1, other)))
    cnt_wait(0, other)
    total = jnp.sum(cnt_recv[...].reshape(blocks, 8, S_BLK), axis=0)
    column = jnp.transpose(jnp.broadcast_to(total[0:1], (S_BLK, S_BLK)))
    column = jnp.maximum(column, 1.0)

    rep_copy(T - 1).wait_recv()
    tsum[T - 1, r] += rep_recv[T - 1].astype(F32)

    def gather_sum(i):
        p = lax.rem(t + i, T)
        remote(z_send.at[0], z_recv.at[p], z_ss.at[0], z_rs.at[p], {"tiles": p}).wait_recv()
        tsum[T - 1, r] += z_recv[p].astype(F32)

    loop(T - 1, lambda k: gather_sum(k + 1))
    sums = tsum[T - 1, r]
    pooled = jnp.concatenate(
        [sums[:, g * 128 : (g + 1) * 128] / column for g in range(wid // 128)], axis=1
    ).astype(BF16)
    pool[f] = pooled

    def feat_copy(ref, ss, rs, i):
        p = lax.rem(f + i, F)
        return remote(ref.at[f], ref.at[f], ss.at[p], rs.at[f], {"feat": p})

    def feat_wait(ref, ss, rs, i):
        p = lax.rem(f + i, F)
        remote(ref.at[p], ref.at[p], ss.at[p], rs.at[p], {"feat": p}).wait_recv()

    for i in range(1, F):
        feat_copy(pool, pool_ss, pool_rs, i).start()
    loads[chunks + 1].wait()
    for load in small:
        load.wait()
    for i in range(1, F):
        feat_wait(pool, pool_ss, pool_rs, i)

    lifted = jnp.concatenate([pool[p].astype(F32) for p in range(F)], axis=1)
    mean = jnp.sum(lifted, axis=1, keepdims=True) * (1.0 / dim)
    centred = lifted - mean
    var = jnp.sum(centred * centred, axis=1, keepdims=True) * (1.0 / dim)
    normed = (centred * lax.rsqrt(var + 1e-05) * gain_ref[...]).astype(BF16)

    same_head = (
        lax.broadcasted_iota(jnp.int32, (wid, wid), 0) // HEAD
        == lax.broadcasted_iota(jnp.int32, (wid, wid), 1) // HEAD
    )
    spread = jnp.where(same_head, 1.0, 0.0).astype(BF16)

    def project(i):
        return jnp.dot(normed, wqkv[i], preferred_element_type=F32)

    def unit(proj):
        square = proj * proj
        high = square.astype(BF16)
        low = (square - high.astype(F32)).astype(BF16)
        norm = jnp.dot(high, spread, preferred_element_type=F32) + jnp.dot(
            low, spread, preferred_element_type=F32
        )
        return (proj * lax.rsqrt(norm + 1e-06)).astype(BF16)

    def inside(offset):
        return (block + offset >= 0) & (block + offset < blocks)

    sib, cross, handed = 2 - r, 1 + r, 3 * (1 - r)
    steps = {0: -1, 3: 1}

    def kv_copy(i, j):
        slot = len(OFFSETS) - 1 - j
        return remote(
            kv_own.at[i], kv_recv.at[slot, i], kv_ss.at[j, i], kv_rs.at[slot, i],
            {"tiles": t + steps[j]},
        )

    def sib_copy(i):
        return remote(
            kv_own.at[i], kv_recv.at[1 + r, i], kv_ss.at[sib, i], kv_rs.at[1 + r, i],
            {"rep": other},
        )

    def hand_copy(i):
        return remote(
            kv_recv.at[handed, i], kv_recv.at[2 - r, i], kv_ss.at[cross, i],
            kv_rs.at[2 - r, i], {"rep": other},
        )

    def kv_wait(i, j):
        remote(
            kv_own.at[i], kv_recv.at[j, i], kv_ss.at[j, i], kv_rs.at[j, i], {"rep": other}
        ).wait_recv()

    def send_kv(i):
        for j in steps:
            @pl.when(inside(OFFSETS[j]))
            def _():
                kv_copy(i, j).start()
        sib_copy(i).start()

    kv_own[0] = unit(project(1))
    send_kv(0)
    kv_own[1] = project(2).astype(BF16)
    send_kv(1)
    query = unit(project(0))
    temper = temper_ref[...]
    lane_head = lax.broadcasted_iota(jnp.int32, (S_BLK, wid), 1) // HEAD
    for h in range(H):
        qm[h * S_BLK : (h + 1) * S_BLK] = jnp.where(lane_head == h, query, jnp.zeros_like(query))

    def attend(keys, values, mask, first):
        scores = lax.dot_general(qm[...], keys, NT, preferred_element_type=F32)
        expd = jnp.concatenate(
            [
                jnp.exp(scores[h * S_BLK : (h + 1) * S_BLK] * temper[:, h : h + 1])
                for h in range(H)
            ],
            axis=0,
        )
        if mask is not None:
            expd = expd * mask
        got = jnp.dot(expd.astype(BF16), values, preferred_element_type=F32)
        if first:
            lsum[...] = expd
            acc[...] = got
        else:
            lsum[...] += expd
            acc[...] += got

    attend(kv_own[0], kv_own[1], None, True)

    def take(j):
        lanes = lax.broadcasted_iota(jnp.int32, adj_ref.shape, 1)
        on = jnp.where((lanes == j) & (adj_ref[...] == 1), 1.0, 0.0)
        mask = jnp.sum(on, axis=1, keepdims=True)
        attend(kv_recv[j, 0], kv_recv[j, 1], mask, False)

    kv_wait(0, sib)
    kv_wait(1, sib)
    take(sib)

    @pl.when(inside(2 - 4 * r))
    def _():
        for i in range(2):
            kv_wait(i, handed)
            hand_copy(i).start()
        take(handed)

    @pl.when(inside(4 * r - 2))
    def _():
        kv_wait(0, 3 - handed)
        kv_wait(1, 3 - handed)
        take(3 - handed)

    @pl.when(inside(2 * r - 1))
    def _():
        kv_wait(0, cross)
        kv_wait(1, cross)
        take(cross)

    attended = jnp.zeros((S_BLK, wid), F32)
    for h in range(H):
        part = slice(h * S_BLK, (h + 1) * S_BLK)
        scale = 1.0 / jnp.sum(lsum[part], axis=1, keepdims=True)
        attended = jnp.where(lane_head == h, acc[part] * scale, attended)
    att[f] = attended.astype(BF16)
    for i in range(1, F):
        feat_copy(att, att_ss, att_rs, i).start()
    loads[chunks + 2].wait()
    mixed = pool[f].astype(F32) + jnp.dot(att[f], wo[f], preferred_element_type=F32)
    for i in range(1, F):
        p = lax.rem(f + i, F)
        remote(wo.at[p], wo.at[p], wo_ss.at[p], wo_rs.at[p], {"feat": p}).wait_recv()
        feat_wait(att, att_ss, att_rs, i)
        mixed += jnp.dot(att[p], wo[p], preferred_element_type=F32)
    out_ref[...] = mixed.astype(out_ref.dtype)

    loop(T - 1, lambda k: (cnt_copy(k + 1, r).wait_send(), cnt_copy(k + 1, other).wait_send()))
    cnt_copy(0, other).wait_send()
    loop(T, lambda k: rep_copy(k).wait_send())
    loop(T - 1, lambda k: z_copy(k).wait_send())
    for i in range(1, F):
        wo_copy(i).wait_send()
        feat_copy(pool, pool_ss, pool_rs, i).wait_send()
        feat_copy(att, att_ss, att_rs, i).wait_send()
    for i in range(2):
        sib_copy(i).wait_send()
    for j in steps:
        @pl.when(inside(OFFSETS[j]))
        def _():
            kv_copy(0, j).wait_send()
            kv_copy(1, j).wait_send()

    @pl.when(inside(2 - 4 * r))
    def _():
        hand_copy(0).wait_send()
        hand_copy(1).wait_send()


def body(points, dest_tile, member, w_point, ln_gain, w_qkv, temper, w_out, adjacency):
    T, R, F = lax.axis_size("tiles"), lax.axis_size("rep"), lax.axis_size("feat")
    H = temper.shape[0]
    rows, dim = points.shape
    wid = w_point.shape[1]
    near = len(OFFSETS)
    vmem = pl.BlockSpec(memory_space=pltpu.VMEM)
    hbm = pl.BlockSpec(memory_space=pl.ANY)
    dma = pltpu.SemaphoreType.DMA
    return pl.pallas_call(
        functools.partial(kernel, T, R, F, H),
        out_shape=jax.ShapeDtypeStruct((S_BLK, wid), BF16),
        in_specs=[hbm] * 9,
        out_specs=vmem,
        scratch_shapes=[
            pltpu.VMEM((1, rows), jnp.int32),
            pltpu.VMEM((1, rows), jnp.int32),
            pltpu.VMEM((1, H), F32),
            pltpu.VMEM(adjacency.shape, jnp.int32),
            pltpu.VMEM((1, dim), F32),
            pltpu.VMEM((rows, dim), BF16),
            pltpu.VMEM((dim, wid), BF16),
            pltpu.VMEM((3, dim, wid), BF16),
            pltpu.VMEM((F, wid, wid), BF16),
            pltpu.VMEM((rows, wid), BF16),
            pltpu.VMEM((R * S_BLK, rows), BF16),
            pltpu.VMEM((T, R, 8, S_BLK), F32),
            pltpu.VMEM((T, R, 8, S_BLK), F32),
            pltpu.VMEM((T, R, S_BLK, wid), F32),
            pltpu.VMEM((T, S_BLK, wid), BF16),
            pltpu.VMEM((T, S_BLK, wid), BF16),
            pltpu.VMEM((T, S_BLK, wid), BF16),
            pltpu.VMEM((T, S_BLK, wid), BF16),
            pltpu.VMEM((F, S_BLK, wid), BF16),
            pltpu.VMEM((2, S_BLK, wid), BF16),
            pltpu.VMEM((near, 2, S_BLK, wid), BF16),
            pltpu.VMEM((F, S_BLK, wid), BF16),
            pltpu.VMEM((H * S_BLK, wid), BF16),
            pltpu.VMEM((H * S_BLK, S_BLK), F32),
            pltpu.VMEM((H * S_BLK, wid), F32),
            dma((rows // CHUNK + 8,)),
            dma((F,)), dma((F,)),
            dma((T, R)), dma((T, R)),
            dma((T,)), dma((T,)),
            dma((T,)), dma((T,)),
            dma((F,)), dma((F,)),
            dma((near, 2)), dma((near, 2)),
            dma((F,)), dma((F,)),
        ],
        compiler_params=pltpu.CompilerParams(
            collective_id=0, has_side_effects=True, vmem_limit_bytes=56000 * 1024
        ),
    )(
        dest_tile.reshape(1, rows), member.reshape(1, rows), temper.reshape(1, H), adjacency,
        ln_gain.reshape(1, dim), points, w_point, w_qkv, w_out,
    )


def solution(mesh):
    return jax.shard_map(
        body,
        mesh=mesh,
        in_specs=(
            P(("groups", "tiles", "rep"), None),
            P(("groups", "tiles", "rep"), None),
            P(("groups", "tiles", "rep")),
            P(None, "feat"),
            P(),
            P(None, None, "feat"),
            P("feat"),
            P("feat", None),
            P(("groups", "tiles", "rep"), None),
        ),
        out_specs=P(("groups", "tiles", "rep"), "feat"),
        check_vma=False,
    )
```
